256 devices in a mesh: node: 256 (over z, x, y, core).
Axes of the slice: x: 4, y: 4, z: 8, core: 2. Of those that a mesh axis runs over, the one named last changes fastest.
Arguments:
- embed: float32 [1048576, 128], P('node')
- tiles: bfloat16 [49152, 128, 128], P('node'), may hold values from -0.21875 to 0.21875
- tile_rows: int32 [49152], P('node'), may hold values from 0 to 31
- tile_cols: int32 [49152], P('node'), may hold values from 0 to 8191, as said below
- tile_count: int32 [256], P('node'), may hold values from 48 to 192, as said below
Outputs:
- spectral: float32 [1048576, 128], P('node')
The draws below stay inside these ranges and needn't reach their ends.
Inputs may be any that keep to these rules, and one draw needn't show every extreme that they name: `tile_cols`: slot s of device d names one of device d's own blocks, one of the last 16 blocks of device d - 1, or one of the first 16 blocks of device d + 1 (devices counted around the cycle); the first slot of every device names a block of device d - 1 and the second one of device d + 1. `tile_count`: some device has all 192 slots live.
All inputs are finite; a program needn't handle non-finite values.
Results may differ from the reference program's by a relative error of at most 0.003.
Values may be sent and summed in bfloat16 or wider, within the bound.
No kernel may reach another device: no remote copies, remote signals or barrier semaphores. Data moves between devices by JAX's collectives and lax.ppermute only.
A program may use at most 128 MiB of HBM per device.

```python
import jax
import jax.numpy as jnp
from jax import lax

BS = 128
DIM = 128
TPB = 6
BLK_DEV = 32
HALO_BLK = 16
TILE_DEV = 192
TILES = 49152
ROWS = 1048576
N_NODE = 256


def draw_embed(key, part):
    key = jax.random.fold_in(key, 1)
    first_key, second_key, third_key = jax.random.split(key, 3)
    total = BLK_DEV * BS * N_NODE
    column_scale = jnp.exp(jax.random.uniform(second_key, (1, DIM), jnp.float32) * jnp.log(10.0))
    device = (jnp.arange(total) // (BLK_DEV * BS)).astype(jnp.float32)
    ramp = 1.0 + 2.0 * device / max(N_NODE - 1, 1)
    base = jax.random.normal(first_key, (total, DIM), jnp.float32)
    rough = jnp.exp(jax.random.uniform(third_key, (total, 1), jnp.float32, -0.7, 0.7))
    return base * column_scale * ramp[:, None] * rough * 0.25


def draw_tile_cols(key, part):
    key = jax.random.fold_in(key, 2)
    first_key, second_key, third_key = jax.random.split(key, 3)
    total = TILE_DEV * N_NODE
    slots = jnp.arange(total, dtype=jnp.int32)
    device = slots // TILE_DEV
    within = slots % TILE_DEV
    kinds = jax.random.randint(first_key, (total,), 0, 4)
    kinds = jnp.where(within == 0, 0, jnp.where(within == 1, 1, kinds))
    edge = jax.random.randint(second_key, (total,), 0, HALO_BLK)
    owned = jax.random.randint(third_key, (total,), 0, BLK_DEV)
    extended = jnp.where(kinds == 0, edge, jnp.where(kinds == 1, HALO_BLK + BLK_DEV + edge, HALO_BLK + owned))
    nblocks = BLK_DEV * N_NODE
    return ((device * BLK_DEV + extended - HALO_BLK) % nblocks).astype(jnp.int32)


def draw_tile_count(key, part):
    key = jax.random.fold_in(key, 3)
    first_key, second_key = jax.random.split(key)
    counts = jax.random.randint(first_key, (N_NODE,), TILE_DEV // 4, TILE_DEV + 1)
    fullest = jax.random.randint(second_key, (), 0, N_NODE)
    return jnp.where(jnp.arange(N_NODE) == fullest, TILE_DEV, counts).astype(jnp.int32)


def plant(values, stream_key, least, top_value):
    shape = values.shape
    spot = [jax.random.randint(jax.random.fold_in(stream_key, axis), (), 0, shape[axis]) for axis in range(len(shape))]
    values = values.at[tuple(spot)].set(least)
    longest = shape.index(max(shape))
    spot[longest] = (spot[longest] + 1) % shape[longest]
    return values.at[tuple(spot)].set(top_value)


def steps_of(own_key, shape, shards, smallest, top_value):
    level = 1.0
    for position, parts in shards:
        draws = jax.random.uniform(jax.random.fold_in(jax.random.fold_in(own_key, 6), position), (parts,), jnp.float32, smallest / len(shards), top_value / len(shards))
        level = level * jnp.repeat(jnp.exp(draws), shape[position] // parts).reshape((-1,) + (1,) * (len(shape) - 1 - position))
    return level


def centred(key, shape, scale, bound, cuts=(), kind=jnp.bfloat16):
    result = jax.random.normal(key, shape, jnp.float32) * scale
    if len(cuts) > 0:
        result = steps_of(key, shape, cuts, -0.22, 0.18) * result
    return jnp.clip(result, min=-bound, max=bound).astype(kind)


def setup_inputs(seed: int = 0) -> dict:
    key_of = jax.random.split(jax.random.key(seed), 6)
    embed = draw_embed(jax.random.fold_in(key_of[5], 71), 0)
    tiles = centred(key_of[1], (TILES, BS, BS), (BS * TPB) ** -0.5, 0.21875, ((0, 256),))
    tile_rows = plant(jax.random.randint(key_of[2], (TILES,), 0, BLK_DEV), jax.random.fold_in(key_of[2], 1), 0, BLK_DEV - 1).astype(jnp.int32)
    tile_cols = draw_tile_cols(jax.random.fold_in(key_of[5], 71), 0)
    tile_count = draw_tile_count(jax.random.fold_in(key_of[5], 71), 0)
    return dict(embed=embed, tiles=tiles, tile_rows=tile_rows, tile_cols=tile_cols, tile_count=tile_count)


spectral_shift = 0.5
weight_zero = 0.6
weight_one = -0.9
weight_two = 0.45

def propagate(field, tiles, tile_rows, tile_cols, tile_count):
    nblocks = BLK_DEV * N_NODE
    rounded = field.astype(jnp.bfloat16).reshape(nblocks, BS, DIM)
    tiles_dev = tiles.reshape(N_NODE, TILE_DEV, BS, BS)
    rows_dev = tile_rows.reshape(N_NODE, TILE_DEV)
    cols_dev = tile_cols.reshape(N_NODE, TILE_DEV)

    def one_device(items):
        tile_set, row_set, col_set, count = items
        picked = jnp.take(rounded, col_set, axis=0)
        product = jnp.einsum('tij,tjf->tif', tile_set.astype(jnp.float32), picked.astype(jnp.float32), precision=lax.Precision.HIGHEST)
        alive = (jnp.arange(TILE_DEV) < count).astype(jnp.float32)
        product = product * alive[:, None, None]
        return jax.ops.segment_sum(product, row_set, num_segments=BLK_DEV)
    summed = lax.map(one_device, (tiles_dev, rows_dev, cols_dev, tile_count))
    return summed.reshape(nblocks * BS, DIM) - spectral_shift * field

def reference(embed, tiles, tile_rows, tile_cols, tile_count):
    first = propagate(embed, tiles, tile_rows, tile_cols, tile_count)
    second = 2.0 * propagate(first, tiles, tile_rows, tile_cols, tile_count) - embed
    mixed = weight_zero * embed + weight_one * first + weight_two * second
    gram = jnp.dot(mixed.T.astype(jnp.float32), mixed.astype(jnp.float32), precision=lax.Precision.HIGHEST, preferred_element_type=jnp.float32)
    lower = jnp.linalg.cholesky(gram)
    solved = jax.scipy.linalg.solve_triangular(lower, mixed.T, lower=True).T
    return solved * jnp.sqrt(jnp.float32(ROWS))
```

```python
import jax
import jax.numpy as jnp
from jax import lax
from jax.experimental import pallas as pl
from jax.experimental.pallas import tpu as pltpu
from jax.sharding import PartitionSpec as P

BS = 128
OWN = 32
HALF = 16
SLOTS = 192
LISTLEN = 256
GROUP = 4
PANEL = 16
MIB = 1024 * 1024

F32 = jnp.float32
BF16 = jnp.bfloat16

spectral_shift = 0.5
weight_zero = 0.6
weight_one = -0.9
weight_two = 0.45
c_embed = weight_zero - weight_two
c_sum = 2.0 * weight_two
c_first = weight_one - c_sum * spectral_shift


def vmem(*shape, dtype):
    return pltpu.VMEM(shape, dtype)


def in_vmem(array):
    return pltpu.with_memory_space_constraint(array, pltpu.VMEM)


V = pl.BlockSpec(memory_space=pltpu.VMEM)
S = pl.BlockSpec(memory_space=pltpu.SMEM)
H = pl.BlockSpec(memory_space=pl.ANY)


def params(mib):
    return pltpu.CompilerParams(vmem_limit_bytes=mib * MIB)


def cost(flops, moved):
    return pl.CostEstimate(flops=flops, bytes_accessed=moved, transcendentals=0)


def slot_lists(tile_rows, tile_cols, tile_count, device, flip, size):
    i32 = jnp.int32
    core = device % 2
    local = (tile_cols - device * OWN + HALF) % (OWN * size)
    own = (local >= HALF) & (local < HALF + OWN)
    after = (local >= HALF + OWN).astype(i32)
    source = jnp.where(own, (local - HALF) ^ flip, local - 48 * after + HALF * (after ^ core))
    row = tile_rows ^ flip
    slots = jnp.arange(SLOTS, dtype=i32)
    alive = slots < tile_count[0]
    bucket = jnp.where(alive, jnp.where(own, row, row + OWN), 2 * OWN)
    code = slots | (source << 8) | (row << 16)
    same = bucket[:, None] == bucket[None, :]
    rank = jnp.sum((same & (slots[None, :] < slots[:, None])).astype(i32), axis=1)
    buckets = jnp.arange(2 * OWN, dtype=i32)
    count = jnp.sum((bucket[None, :] == buckets[:, None]).astype(i32), axis=1)
    pairs = (count + 1) // 2
    earlier = (buckets[None, :] < bucket[:, None]) & ((buckets[None, :] >= OWN) == (bucket[:, None] >= OWN))
    start = jnp.sum(jnp.where(earlier, 2 * pairs[None, :], 0), axis=1)
    place = jnp.where(alive, start + rank + jnp.where(bucket >= OWN, LISTLEN, 0), -1)
    places = jnp.arange(2 * LISTLEN, dtype=i32)
    hit = place[None, :] == places[:, None]
    order = SLOTS + jnp.sum(jnp.where(hit, code[None, :] - SLOTS, 0), axis=1)
    n_own = jnp.sum(pairs[:OWN])
    n_cross = jnp.sum(pairs[OWN : OWN + HALF])
    n_halo = jnp.sum(pairs[OWN:])
    meta = jnp.stack([flip, n_own, n_cross, n_halo]).astype(i32)
    return order, meta


def tile_sums(order, start, stop, source, tiles, total):
    def group(g, carry):
        products = []
        for u in range(GROUP):
            at = start + 2 * (g * GROUP + u)
            first, second = order[at], order[at + 1]
            wide = jnp.concatenate([tiles[first & 255], tiles[second & 255]], axis=1)
            tall = jnp.concatenate([source[(first >> 8) & 255], source[(second >> 8) & 255]], axis=0)
            products.append((first >> 16, jnp.dot(wide, tall, preferred_element_type=F32)))
        for row, product in products:
            total[row] += product
        return carry

    lax.fori_loop(0, (stop + GROUP - 1) // GROUP, group, 0)


def own_first_kernel(order, meta, cross, inner, embed, tiles, total, kept, source, sem):
    flip = meta[0]
    halves = [
        pltpu.make_async_copy(
            embed.at[pl.ds(h * HALF ^ flip, HALF)], total.at[pl.ds(h * HALF, HALF)], sem.at[h]
        )
        for h in range(2)
    ]
    tile_copy = pltpu.make_async_copy(tiles, kept.at[pl.ds(0, SLOTS)], sem.at[2])
    for copy in halves:
        copy.start()
    tile_copy.start()
    kept[SLOTS] = jnp.zeros((BS, BS), BF16)
    source[:HALF] = cross[...]
    source[HALF:] = inner[...]
    for copy in halves:
        copy.wait()
    total[...] = total[...] * (-spectral_shift)
    tile_copy.wait()
    tile_sums(order, 0, meta[1], source, kept, total)


def halo_first_kernel(order, meta, cross, inner, tiles, before, total, out_cross, out_inner, source):
    source[:HALF] = cross[...]
    source[HALF:] = inner[...]
    total[...] = before[...]
    tile_sums(order, LISTLEN, meta[3], source, tiles, total)
    out_cross[...] = total[:HALF].astype(BF16)
    out_inner[...] = total[HALF:].astype(BF16)


def own_second_kernel(order, meta, cross, inner, tiles, first, total, source):
    source[:HALF] = cross[...]
    source[HALF:] = inner[...]
    total[...] = first[...] * (c_first / c_sum)
    tile_sums(order, 0, meta[1], source, tiles, total)


def halo_second_kernel(order, meta, cross, inner, tiles, before, embed, split, gram, source, total, field, sem):
    flip = meta[0]
    halves = [
        pltpu.make_async_copy(
            embed.at[pl.ds(h * HALF ^ flip, HALF)], field.at[pl.ds(h * HALF, HALF)], sem.at[h]
        )
        for h in range(2)
    ]
    for copy in halves:
        copy.start()
    source[:HALF] = cross[...]
    source[HALF:] = inner[...]
    total[...] = before[...]
    tile_sums(order, LISTLEN, meta[3], source, tiles, total)
    for copy in halves:
        copy.wait()

    def block(g, sums):
        mixed = c_sum * total[pl.ds(2 * g, 2)] + c_embed * field[pl.ds(2 * g, 2)]
        mixed = mixed.reshape(2 * BS, BS)
        high = mixed.astype(BF16)
        low = (mixed - high.astype(F32)).astype(BF16)
        both = jnp.concatenate([high, low], axis=1)
        split[g] = both
        return sums + lax.dot_general(high, both, (((0,), (0,)), ((), ())), preferred_element_type=F32)

    sums = lax.fori_loop(0, OWN // 2, block, jnp.zeros((BS, 2 * BS), F32))
    gram[...] = sums[:, :BS] + (sums[:, BS:] + sums[:, BS:].T)


def three_parts(x):
    high = x.astype(BF16)
    rest = x - high.astype(F32)
    middle = rest.astype(BF16)
    low = (rest - middle.astype(F32)).astype(BF16)
    return high, middle, low


def inverse_factor(gram, work):
    n = BS
    rows = lax.broadcasted_iota(jnp.int32, (n, n), 0)
    columns = lax.broadcasted_iota(jnp.int32, (n, n), 1)
    work[:, :n] = gram
    work[:, n:] = jnp.where(rows == columns, 1.0, 0.0).astype(F32)
    place = lax.broadcasted_iota(jnp.int32, (PANEL, n), 0)
    for base in range(0, n, PANEL):
        panel = work[base : base + PANEL, :]
        left, right = panel[:, :n], panel[:, n:]
        spread = [
            jnp.broadcast_to(left[:, base + k : base + k + 1], (PANEL, n)) for k in range(PANEL)
        ]
        scale = jnp.zeros((PANEL, n), F32)
        for j in range(PANEL):
            inverse = 1.0 / spread[j][j : j + 1, :]
            scale = jnp.where(place == j, inverse, scale)
            if j + 1 < PANEL:
                factor = jnp.where(place > j, spread[j] * inverse, 0.0)
                for k in range(j + 1, PANEL):
                    spread[k] = spread[k] - factor * spread[k][j : j + 1, :]
                left = left - factor * left[j : j + 1, :]
                right = right - factor * right[j : j + 1, :]
        if base + PANEL < n:
            ah, am, al = three_parts(left * scale)
            both = jnp.concatenate([left, right], axis=1)
            bh, bm, bl = three_parts(both)
            update = lax.dot_general(
                jnp.concatenate([ah, ah, am, am, ah, al], axis=0),
                jnp.concatenate([bh, bm, bh, bm, bl, bh], axis=0),
                (((0,), (0,)), ((), ())),
                preferred_element_type=F32,
            )
            work[base + PANEL :, :] -= update[base + PANEL :, :]
        work[base : base + PANEL, n:] = right * jnp.sqrt(scale)


def solve_kernel(total_rows, meta, gram, split, out, work, result, sem):
    flip = meta[0]
    inverse_factor(gram[...], work)
    spread = (work[:, BS:] * jnp.sqrt(F32(total_rows))).T
    high = spread.astype(BF16)
    low = (spread - high.astype(F32)).astype(BF16)
    half = jnp.concatenate([high, low], axis=1)
    factor = jnp.concatenate([half, half], axis=0)
    steps = 8
    size = OWN // steps
    copies = []
    for step in range(steps):
        rows = split[step * size // 2 : (step + 1) * size // 2].reshape(size * BS, 2 * BS)
        product = jnp.dot(rows, factor, preferred_element_type=F32)
        result[step * size : (step + 1) * size] = (product[:, :BS] + product[:, BS:]).reshape(size, BS, BS)
        copies.append(
            pltpu.make_async_copy(
                result.at[pl.ds(step * size, size)], out.at[pl.ds(step * size ^ flip, size)], sem.at[step]
            )
        )
        copies[-1].start()
    for copy in copies:
        copy.wait()


def swap(pairs, x):
    return lax.ppermute(x, "node", pairs)


def sum_over_node(x, size):
    step = 1
    while step < size:
        x = x + swap([(i, i ^ step) for i in range(size)], x)
        step *= 2
    return x


def local(embed, tiles, tile_rows, tile_cols, tile_count):
    size = lax.axis_size("node")
    device = lax.axis_index("node")
    flip = (device % 2) * HALF
    to_chip = [(i, (i + 1) % size if i % 2 else (i - 1) % size) for i in range(size)]
    to_core = [(i, i ^ 1) for i in range(size)]
    blocks = embed.reshape(OWN, BS, BS)

    cross = lax.dynamic_slice_in_dim(blocks, flip, HALF, 0).astype(BF16)
    cross_in = swap(to_chip, cross)
    inner = lax.dynamic_slice_in_dim(blocks, HALF - flip, HALF, 0).astype(BF16)
    inner_in = swap(to_core, inner)
    order, meta = slot_lists(tile_rows, tile_cols, tile_count, device, flip, size)

    blocks_f32 = vmem(OWN, BS, BS, dtype=F32)
    source = vmem(OWN, BS, BS, dtype=BF16)
    half = vmem(HALF, BS, BS, dtype=BF16)
    work = cost(2 * 96 * BS**3, 8 * MIB)
    total, kept = pl.pallas_call(
        own_first_kernel,
        out_shape=(blocks_f32, vmem(SLOTS + 1, BS, BS, dtype=BF16)),
        in_specs=[S, S, V, V, H, H],
        out_specs=(V, V),
        scratch_shapes=[source, pltpu.SemaphoreType.DMA((3,))],
        compiler_params=params(24),
        cost_estimate=work,
        name="own_first",
    )(order, meta, in_vmem(cross), in_vmem(inner), blocks, tiles)

    first, cross, inner = pl.pallas_call(
        halo_first_kernel,
        out_shape=(blocks_f32, half, half),
        in_specs=[S, S, V, V, V, V],
        out_specs=(V, V, V),
        scratch_shapes=[source],
        compiler_params=params(24),
        cost_estimate=work,
        name="halo_first",
    )(order, meta, in_vmem(cross_in), in_vmem(inner_in), in_vmem(kept), in_vmem(total))

    cross_in = swap(to_chip, cross)
    inner_in = swap(to_core, inner)
    total = pl.pallas_call(
        own_second_kernel,
        out_shape=blocks_f32,
        in_specs=[S, S, V, V, V, V],
        out_specs=V,
        scratch_shapes=[source],
        compiler_params=params(24),
        cost_estimate=work,
        name="own_second",
    )(order, meta, in_vmem(cross), in_vmem(inner), in_vmem(kept), in_vmem(first))

    split, gram = pl.pallas_call(
        halo_second_kernel,
        out_shape=(vmem(OWN // 2, 2 * BS, 2 * BS, dtype=BF16), vmem(BS, BS, dtype=F32)),
        in_specs=[S, S, V, V, V, V, H],
        out_specs=(V, V),
        scratch_shapes=[source, blocks_f32, blocks_f32, pltpu.SemaphoreType.DMA((2,))],
        compiler_params=params(24),
        cost_estimate=work,
        name="halo_second",
    )(order, meta, in_vmem(cross_in), in_vmem(inner_in), in_vmem(kept), in_vmem(total), blocks)

    gram = sum_over_node(gram, size)

    def solve(*refs):
        solve_kernel(embed.shape[0] * size, *refs)

    out = pl.pallas_call(
        solve,
        out_shape=jax.ShapeDtypeStruct((OWN, BS, BS), F32),
        in_specs=[S, V, V],
        out_specs=H,
        scratch_shapes=[vmem(BS, 2 * BS, dtype=F32), blocks_f32, pltpu.SemaphoreType.DMA((8,))],
        compiler_params=params(24),
        name="solve",
    )(meta, in_vmem(gram), in_vmem(split))
    return out.reshape(embed.shape)


def solution(mesh):
    return jax.shard_map(
        local,
        mesh=mesh,
        in_specs=(P("node", None), P("node", None, None), P("node"), P("node"), P("node")),
        out_specs=P("node", None),
        check_vma=False,
    )
```

```python
import jax
import jax.numpy as jnp
from jax import lax
from jax.experimental import pallas as pl
from jax.experimental.pallas import tpu as pltpu
from jax.sharding import PartitionSpec as P

BS = 128
OWN = 32
HALF = 16
SLOTS = 192
LISTLEN = 256
GROUP = 4
PANEL = 16
TILE_COPIES = 8
CHUNK = 4
LOW = BS // 2
MIB = 1024 * 1024

F32 = jnp.float32
BF16 = jnp.bfloat16

spectral_shift = 0.5
weight_zero = 0.6
weight_one = -0.9
weight_two = 0.45
c_embed = weight_zero - weight_two
c_sum = 2.0 * weight_two
c_first = weight_one - c_sum * spectral_shift


def vmem(*shape, dtype):
    return pltpu.VMEM(shape, dtype)


def in_vmem(array):
    return pltpu.with_memory_space_constraint(array, pltpu.VMEM)


V = pl.BlockSpec(memory_space=pltpu.VMEM)
S = pl.BlockSpec(memory_space=pltpu.SMEM)
H = pl.BlockSpec(memory_space=pl.ANY)
M = pl.BlockSpec(memory_space=pltpu.HBM)


def params(mib):
    return pltpu.CompilerParams(vmem_limit_bytes=mib * MIB)


def cost(flops, moved):
    return pl.CostEstimate(flops=flops, bytes_accessed=moved, transcendentals=0)


def slot_lists(tile_rows, tile_cols, tile_count, device, flip, size):
    i32 = jnp.int32
    core = device % 2
    local = (tile_cols - device * OWN + HALF) % (OWN * size)
    own = (local >= HALF) & (local < HALF + OWN)
    after = (local >= HALF + OWN).astype(i32)
    source = jnp.where(own, (local - HALF) ^ flip, local - 48 * after + HALF * (after ^ core))
    row = tile_rows ^ flip
    slots = jnp.arange(SLOTS, dtype=i32)
    alive = slots < tile_count[0]
    bucket = jnp.where(alive, jnp.where(own, row, row + OWN), 2 * OWN)
    code = slots | (source << 8) | (row << 16)
    same = bucket[:, None] == bucket[None, :]
    rank = jnp.sum((same & (slots[None, :] < slots[:, None])).astype(i32), axis=1)
    buckets = jnp.arange(2 * OWN, dtype=i32)
    count = jnp.sum((bucket[None, :] == buckets[:, None]).astype(i32), axis=1)
    pairs = (count + 1) // 2
    earlier = (buckets[None, :] < bucket[:, None]) & ((buckets[None, :] >= OWN) == (bucket[:, None] >= OWN))
    start = jnp.sum(jnp.where(earlier, 2 * pairs[None, :], 0), axis=1)
    place = jnp.where(alive, start + rank + jnp.where(bucket >= OWN, LISTLEN, 0), -1)
    places = jnp.arange(2 * LISTLEN, dtype=i32)
    hit = place[None, :] == places[:, None]
    order = SLOTS + jnp.sum(jnp.where(hit, code[None, :] - SLOTS, 0), axis=1)
    field = jnp.arange(8, dtype=i32)[:, None]
    counted = (buckets[None, :] < OWN) == (field == 1)
    meta = jnp.sum(jnp.where(counted, pairs[None, :], 0), axis=1)
    return order, jnp.where(field[:, 0] == 0, flip, meta)


def tile_sums(order, start, stop, source, tiles, total):
    def group(g, carry):
        products = []
        for u in range(GROUP):
            at = start + 2 * (g * GROUP + u)
            first, second = order[at], order[at + 1]
            wide = jnp.concatenate([tiles[first & 255], tiles[second & 255]], axis=1)
            tall = jnp.concatenate([source[(first >> 8) & 255], source[(second >> 8) & 255]], axis=0)
            products.append((first >> 16, jnp.dot(wide, tall, preferred_element_type=F32)))
        for row, product in products:
            total[row] += product
        return carry

    lax.fori_loop(0, (stop + GROUP - 1) // GROUP, group, 0)


def own_first_kernel(order, meta, cross, inner, embed, tiles, total, kept, source, sem):
    flip = meta[0]
    halves = [
        pltpu.make_async_copy(
            embed.at[pl.ds(h * HALF ^ flip, HALF)], total.at[pl.ds(h * HALF, HALF)], sem.at[h]
        )
        for h in range(2)
    ]
    size = SLOTS // TILE_COPIES
    tile_copies = [
        pltpu.make_async_copy(
            tiles.at[pl.ds(c * size, size)], kept.at[pl.ds(c * size, size)], sem.at[2 + c]
        )
        for c in range(TILE_COPIES)
    ]
    for copy in halves + tile_copies:
        copy.start()
    kept[SLOTS] = jnp.zeros((BS, BS), BF16)
    source[:HALF] = cross[...]
    source[HALF:] = inner[...]
    for copy in halves:
        copy.wait()
    total[...] = total[...] * (-spectral_shift)
    for copy in tile_copies:
        copy.wait()
    tile_sums(order, 0, meta[1], source, kept, total)


def halo_first_kernel(order, meta, cross, inner, tiles, before, total, out_cross, out_inner, source):
    source[:HALF] = cross[...]
    source[HALF:] = inner[...]
    tile_sums(order, LISTLEN, meta[2], source, tiles, total)
    out_cross[...] = total[:HALF].astype(BF16)
    out_inner[...] = total[HALF:].astype(BF16)


def own_second_kernel(order, meta, cross, inner, tiles, first, total, source):
    source[:HALF] = cross[...]
    source[HALF:] = inner[...]
    total[...] = total[...] * (c_first / c_sum)
    tile_sums(order, 0, meta[1], source, tiles, total)


def halo_second_kernel(order, meta, cross, inner, tiles, before, embed, split, gram, source, total, field, sem):
    flip = meta[0]
    halves = [
        pltpu.make_async_copy(
            embed.at[pl.ds(h * HALF ^ flip, HALF)], field.at[pl.ds(h * HALF, HALF)], sem.at[h]
        )
        for h in range(2)
    ]
    for copy in halves:
        copy.start()
    source[:HALF] = cross[...]
    source[HALF:] = inner[...]
    total[...] = before[...]
    tile_sums(order, LISTLEN, meta[2], source, tiles, total)
    for copy in halves:
        copy.wait()

    sums = jnp.zeros((BS, 2 * BS), F32)
    for g in range(OWN // CHUNK):
        rows = pl.ds(g * CHUNK, CHUNK)
        mixed = (c_sum * total[rows] + c_embed * field[rows]).reshape(CHUNK * BS, BS)
        high = mixed.astype(BF16)
        low = (mixed - high.astype(F32)).astype(BF16)
        both = jnp.concatenate([high, low], axis=1)
        split[rows] = both.reshape(CHUNK, BS, 2 * BS)
        sums += lax.dot_general(high, both, (((0,), (0,)), ((), ())), preferred_element_type=F32)
    gram[...] = packed(sums[:, :BS] + (sums[:, BS:] + sums[:, BS:].T))


def packed(gram):
    row = lax.broadcasted_iota(jnp.int32, (LOW, BS), 0)
    column = lax.broadcasted_iota(jnp.int32, (LOW, BS), 1)
    lower = pltpu.roll(gram[LOW:], LOW, 1)
    body = jnp.where((column >= LOW) | (row <= column), gram[:LOW], lower)
    diagonal = jnp.sum(jnp.where(row == column, lower, 0.0), axis=0, keepdims=True)
    return jnp.concatenate([body, jnp.broadcast_to(diagonal, (8, BS))], axis=0)


def unpacked(pack):
    row = lax.broadcasted_iota(jnp.int32, (LOW, BS), 0)
    column = lax.broadcasted_iota(jnp.int32, (LOW, BS), 1)
    body = pack[:LOW]
    turned = jnp.concatenate([body, jnp.zeros((LOW, BS), F32)], axis=0).T
    upper = jnp.where((column >= LOW) | (row <= column), body, turned[:LOW])
    lower = jnp.where(row > column, body, jnp.where(row == column, pack[LOW : LOW + 1], turned[:LOW]))
    lower = jnp.where(column < LOW, turned[LOW:], pltpu.roll(lower, LOW, 1))
    return jnp.concatenate([upper, lower], axis=0)


def three_parts(x):
    high = x.astype(BF16)
    rest = x - high.astype(F32)
    middle = rest.astype(BF16)
    low = (rest - middle.astype(F32)).astype(BF16)
    return high, middle, low


def inverse_factor(gram, work):
    n = BS
    rows = lax.broadcasted_iota(jnp.int32, (n, n), 0)
    columns = lax.broadcasted_iota(jnp.int32, (n, n), 1)
    work[:, :n] = gram
    work[:, n:] = jnp.where(rows == columns, 1.0, 0.0).astype(F32)
    place = lax.broadcasted_iota(jnp.int32, (PANEL, n), 0)
    for base in range(0, n, PANEL):
        panel = work[base : base + PANEL, :]
        left, right = panel[:, :n], panel[:, n:]
        spread = [
            jnp.broadcast_to(left[:, base + k : base + k + 1], (PANEL, n)) for k in range(PANEL)
        ]
        scale = jnp.zeros((PANEL, n), F32)
        for j in range(PANEL):
            inverse = 1.0 / spread[j][j : j + 1, :]
            scale = jnp.where(place == j, inverse, scale)
            if j + 1 < PANEL:
                factor = jnp.where(place > j, spread[j] * inverse, 0.0)
                for k in range(j + 1, PANEL):
                    spread[k] = spread[k] - factor * spread[k][j : j + 1, :]
                left = left - factor * left[j : j + 1, :]
                right = right - factor * right[j : j + 1, :]
        if base + PANEL < n:
            ah, am, al = three_parts(left * scale)
            both = jnp.concatenate([left, right], axis=1)
            bh, bm, bl = three_parts(both)
            update = lax.dot_general(
                jnp.concatenate([ah, ah, am, am, ah, al], axis=0),
                jnp.concatenate([bh, bm, bh, bm, bl, bh], axis=0),
                (((0,), (0,)), ((), ())),
                preferred_element_type=F32,
            )
            work[base + PANEL :, :] -= update[base + PANEL :, :]
        work[base : base + PANEL, n:] = right * jnp.sqrt(scale)


def solve_kernel(total_rows, meta, gram, split, out, work, result, sem):
    flip = meta[0]
    inverse_factor(unpacked(gram[...]), work)
    spread = (work[:, BS:] * jnp.sqrt(F32(total_rows))).T
    high = spread.astype(BF16)
    low = (spread - high.astype(F32)).astype(BF16)
    half = jnp.concatenate([high, low], axis=1)
    factor = jnp.concatenate([half, half], axis=0)
    steps = 8
    size = OWN // steps
    copies = []
    for step in range(steps):
        rows = split[step * size : (step + 1) * size].reshape(size * BS, 2 * BS)
        product = jnp.dot(rows, factor, preferred_element_type=F32)
        result[step * size : (step + 1) * size] = (product[:, :BS] + product[:, BS:]).reshape(size, BS, BS)
        copies.append(
            pltpu.make_async_copy(
                result.at[pl.ds(step * size, size)], out.at[pl.ds(step * size ^ flip, size)], sem.at[step]
            )
        )
        copies[-1].start()
    for copy in copies:
        copy.wait()


def swap(pairs, x):
    return lax.ppermute(x, "node", pairs)


def sum_over_node(x, size):
    for masks in ((1,), (2, 6, 4), (8, 24, 16), (32, 64, 96), (224,)):
        x = x + sum(swap([(i, i ^ mask) for i in range(size)], x) for mask in masks)
    return x


def local(embed, tiles, tile_rows, tile_cols, tile_count):
    size = lax.axis_size("node")
    device = lax.axis_index("node")
    flip = (device % 2) * HALF
    to_chip = [(i, (i + 1) % size if i % 2 else (i - 1) % size) for i in range(size)]
    to_core = [(i, i ^ 1) for i in range(size)]
    blocks = embed.reshape(OWN, BS, BS)

    cross = lax.dynamic_slice_in_dim(blocks, flip, HALF, 0).astype(BF16)
    cross_in = swap(to_chip, cross)
    inner = lax.dynamic_slice_in_dim(blocks, HALF - flip, HALF, 0).astype(BF16)
    inner_in = swap(to_core, inner)
    order, meta = slot_lists(tile_rows, tile_cols, tile_count, device, flip, size)

    blocks_f32 = vmem(OWN, BS, BS, dtype=F32)
    source = vmem(OWN, BS, BS, dtype=BF16)
    half = vmem(HALF, BS, BS, dtype=BF16)
    work = cost(2 * 96 * BS**3, 8 * MIB)
    total, kept = pl.pallas_call(
        own_first_kernel,
        out_shape=(blocks_f32, vmem(SLOTS + 1, BS, BS, dtype=BF16)),
        in_specs=[S, S, V, V, M, M],
        out_specs=(V, V),
        scratch_shapes=[source, pltpu.SemaphoreType.DMA((2 + TILE_COPIES,))],
        compiler_params=params(24),
        cost_estimate=work,
        name="own_first",
    )(order, meta, in_vmem(cross), in_vmem(inner), blocks, tiles)

    first, cross, inner = pl.pallas_call(
        halo_first_kernel,
        out_shape=(blocks_f32, half, half),
        in_specs=[S, S, V, V, V, V],
        out_specs=(V, V, V),
        input_output_aliases={5: 0},
        scratch_shapes=[source],
        compiler_params=params(24),
        cost_estimate=work,
        name="halo_first",
    )(order, meta, in_vmem(cross_in), in_vmem(inner_in), in_vmem(kept), in_vmem(total))

    cross_in = swap(to_chip, cross)
    inner_in = swap(to_core, inner)
    total = pl.pallas_call(
        own_second_kernel,
        out_shape=blocks_f32,
        in_specs=[S, S, V, V, V, V],
        out_specs=V,
        input_output_aliases={5: 0},
        scratch_shapes=[source],
        compiler_params=params(24),
        cost_estimate=work,
        name="own_second",
    )(order, meta, in_vmem(cross), in_vmem(inner), in_vmem(kept), in_vmem(first))

    split, gram = pl.pallas_call(
        halo_second_kernel,
        out_shape=(vmem(OWN, BS, 2 * BS, dtype=BF16), vmem(LOW + 8, BS, dtype=F32)),
        in_specs=[S, S, V, V, V, V, M],
        out_specs=(V, V),
        scratch_shapes=[source, blocks_f32, blocks_f32, pltpu.SemaphoreType.DMA((2,))],
        compiler_params=params(24),
        cost_estimate=work,
        name="halo_second",
    )(order, meta, in_vmem(cross_in), in_vmem(inner_in), in_vmem(kept), in_vmem(total), blocks)

    gram = sum_over_node(gram, size)

    def solve(*refs):
        solve_kernel(embed.shape[0] * size, *refs)

    out = pl.pallas_call(
        solve,
        out_shape=jax.ShapeDtypeStruct((OWN, BS, BS), F32),
        in_specs=[S, V, V],
        out_specs=H,
        scratch_shapes=[vmem(BS, 2 * BS, dtype=F32), blocks_f32, pltpu.SemaphoreType.DMA((8,))],
        compiler_params=params(24),
        name="solve",
    )(meta, in_vmem(gram), in_vmem(split))
    return out.reshape(embed.shape)


def solution(mesh):
    return jax.shard_map(
        local,
        mesh=mesh,
        in_specs=(P("node", None), P("node", None, None), P("node"), P("node"), P("node")),
        out_specs=P("node", None),
        check_vma=False,
    )
```

```python
import jax
import jax.numpy as jnp
from jax import lax
from jax.experimental import pallas as pl
from jax.experimental.pallas import tpu as pltpu
from jax.sharding import PartitionSpec as P

BS = 128
OWN = 32
HALF = 16
SLOTS = 192
LISTLEN = 256
GROUP = 4
PANEL = 16
TILE_COPIES = 8
CHUNK = 4
LOW = BS // 2
MIB = 1024 * 1024

F32 = jnp.float32
BF16 = jnp.bfloat16

spectral_shift = 0.5
weight_zero = 0.6
weight_one = -0.9
weight_two = 0.45
c_embed = weight_zero - weight_two
c_sum = 2.0 * weight_two
c_first = weight_one - c_sum * spectral_shift


def vmem(*shape, dtype):
    return pltpu.VMEM(shape, dtype)


def in_vmem(array):
    return pltpu.with_memory_space_constraint(array, pltpu.VMEM)


def in_hbm(array):
    return pltpu.with_memory_space_constraint(array, pltpu.HBM)


V = pl.BlockSpec(memory_space=pltpu.VMEM)
S = pl.BlockSpec(memory_space=pltpu.SMEM)
H = pl.BlockSpec(memory_space=pl.ANY)
M = pl.BlockSpec(memory_space=pltpu.HBM)


def params(mib):
    return pltpu.CompilerParams(vmem_limit_bytes=mib * MIB)


def cost(flops, moved):
    return pl.CostEstimate(flops=flops, bytes_accessed=moved, transcendentals=0)


def which_list(bucket):
    return (bucket >= OWN).astype(jnp.int32) + (bucket >= OWN + HALF).astype(jnp.int32)


def columns_of(row):
    return jnp.broadcast_to(row, (row.shape[1], row.shape[1])).T


def slot_lists(tile_rows, tile_cols, device, count, flip, size):
    i32 = jnp.int32
    shape = (1, LISTLEN)
    core = device % 2
    local = tile_cols - device * OWN + HALF
    local = jnp.where(local < 0, local + OWN * size, local)
    local = jnp.where(local >= OWN * size, local - OWN * size, local)
    own = (local >= HALF) & (local < HALF + OWN)
    after = (local >= HALF + OWN).astype(i32)
    source = jnp.where(own, (local - HALF) ^ flip, local - 48 * after + HALF * (after ^ core))
    row = tile_rows ^ flip
    slots = lax.broadcasted_iota(i32, shape, 1)
    alive = slots < count
    bucket = jnp.where(alive, jnp.where(own, row, row + OWN), 2 * OWN)
    kind = which_list(bucket)
    code = (slots | (source << 8) | (row << 16)).astype(F32)

    square = (LISTLEN, LISTLEN)
    before = lax.broadcasted_iota(i32, square, 0) < lax.broadcasted_iota(i32, square, 1)
    bucket_f32 = bucket.astype(F32)
    same = columns_of(bucket_f32) == jnp.broadcast_to(bucket_f32, square)
    rank = jnp.sum(jnp.where(same & before, 1.0, 0.0), axis=0, keepdims=True)
    wide = (2 * OWN, LISTLEN)
    buckets = lax.broadcasted_iota(i32, wide, 0)
    here = jnp.broadcast_to(bucket, wide)
    pairs = jnp.sum(jnp.where(buckets == here, 1.0, 0.0), axis=1, keepdims=True)
    pairs = jnp.floor((pairs + 1.0) * 0.5)
    kinds = which_list(buckets)
    earlier = (buckets < here) & (kinds == jnp.broadcast_to(kind, wide))
    start = jnp.sum(jnp.where(earlier, 2.0 * pairs, 0.0), axis=0, keepdims=True)
    place = jnp.where(alive, start + rank + (kind * LISTLEN).astype(F32), -1.0)
    place, code = columns_of(place), columns_of(code)
    lanes = lax.broadcasted_iota(i32, square, 1).astype(F32)
    order = [
        SLOTS + jnp.sum(jnp.where(place == lanes + k * LISTLEN, code - SLOTS, 0.0), axis=0, keepdims=True)
        for k in range(3)
    ]
    field = lax.broadcasted_iota(i32, wide, 1)
    meta = jnp.sum(jnp.where(kinds == field - 1, pairs, 0.0), axis=0, keepdims=True)
    meta = jnp.where(slots == 0, flip, meta.astype(i32))
    return jnp.concatenate(order, axis=1).astype(i32), meta


def tile_sums(order, start, stop, source, tiles, total):
    def group(g, carry):
        products = []
        for u in range(GROUP):
            at = start + 2 * (g * GROUP + u)
            first, second = order[0, at], order[0, at + 1]
            wide = jnp.concatenate([tiles[first & 255], tiles[second & 255]], axis=1)
            tall = jnp.concatenate([source[(first >> 8) & 255], source[(second >> 8) & 255]], axis=0)
            products.append((first >> 16, jnp.dot(wide, tall, preferred_element_type=F32)))
        for row, product in products:
            total[row] += product
        return carry

    lax.fori_loop(0, (stop + GROUP - 1) // GROUP, group, 0)


def load_kernel(size, where, counts, rows, columns, embed, tiles, total, kept, inner, order, meta, slots, near_rows, near_columns, sem):
    device, count = where[0], counts[0]
    flip = (device % 2) * HALF
    part = SLOTS // TILE_COPIES
    tile_copies = [
        pltpu.make_async_copy(
            tiles.at[pl.ds(c * part, part)], kept.at[pl.ds(c * part, part)], sem.at[2 + c]
        )
        for c in range(TILE_COPIES)
    ]
    halves = [
        pltpu.make_async_copy(
            embed.at[pl.ds(h * HALF ^ flip, HALF)], total.at[pl.ds(h * HALF, HALF)], sem.at[h]
        )
        for h in range(2)
    ]
    slot_copies = [
        pltpu.make_async_copy(rows, near_rows, sem.at[2 + TILE_COPIES]),
        pltpu.make_async_copy(columns, near_columns, sem.at[3 + TILE_COPIES]),
    ]
    for copy in slot_copies + halves + tile_copies:
        copy.start()
    kept[SLOTS] = jnp.zeros((BS, BS), BF16)
    slots[...] = jnp.zeros_like(slots)
    for copy in slot_copies:
        copy.wait()
    slots[0:1, :SLOTS] = near_rows[...]
    slots[1:2, :SLOTS] = near_columns[...]
    order[...], meta[...] = slot_lists(slots[0:1, :], slots[1:2, :], device, count, flip, size)
    for copy in halves:
        copy.wait()
    inner[...] = total[HALF:].astype(BF16)
    total[...] = total[...] * (-spectral_shift)
    for copy in tile_copies:
        copy.wait()


def own_first_kernel(order, meta, cross, inner, tiles, before, total, source):
    source[:HALF] = cross[...]
    source[HALF:] = inner[...]
    tile_sums(order, 0, meta[0, 1], source, tiles, total)


def halo_first_cross_kernel(order, meta, cross, inner, tiles, before, total, source, out_cross):
    source[:HALF] = cross[...]
    source[HALF:] = inner[...]
    tile_sums(order, LISTLEN, meta[0, 2], source, tiles, total)
    out_cross[...] = total[:HALF].astype(BF16)


def own_second_kernel(order, meta, halo, cross, tiles, before, total, out_lower, out_upper, source):
    tile_sums(order, 2 * LISTLEN, meta[0, 3], halo, tiles, total)
    inner = total[HALF:].astype(BF16)
    out_lower[...] = inner[: HALF // 2]
    out_upper[...] = inner[HALF // 2 :]
    source[:HALF] = cross[...]
    source[HALF:] = inner
    total[...] = total[...] * (c_first / c_sum)
    tile_sums(order, 0, meta[0, 1], source, tiles, total)


def halo_second_kernel(order, meta, cross, lower, upper, tiles, before, embed, split, gram, source, total, field, sem):
    flip = meta[0, 0]
    halves = [
        pltpu.make_async_copy(
            embed.at[pl.ds(h * HALF ^ flip, HALF)], field.at[pl.ds(h * HALF, HALF)], sem.at[h]
        )
        for h in range(2)
    ]
    for copy in halves:
        copy.start()
    source[:HALF] = cross[...]
    source[HALF : HALF + HALF // 2] = lower[...]
    source[HALF + HALF // 2 :] = upper[...]
    total[...] = before[...]
    tile_sums(order, LISTLEN, meta[0, 2], source, tiles, total)
    tile_sums(order, 2 * LISTLEN, meta[0, 3], source, tiles, total)
    for copy in halves:
        copy.wait()

    sums = jnp.zeros((BS, 2 * BS), F32)
    for g in range(OWN // CHUNK):
        rows = pl.ds(g * CHUNK, CHUNK)
        mixed = (c_sum * total[rows] + c_embed * field[rows]).reshape(CHUNK * BS, BS)
        high = mixed.astype(BF16)
        low = (mixed - high.astype(F32)).astype(BF16)
        both = jnp.concatenate([high, low], axis=1)
        split[rows] = both.reshape(CHUNK, BS, 2 * BS)
        sums += lax.dot_general(high, both, (((0,), (0,)), ((), ())), preferred_element_type=F32)
    gram[...] = packed(sums[:, :BS] + (sums[:, BS:] + sums[:, BS:].T))


def packed(gram):
    row = lax.broadcasted_iota(jnp.int32, (LOW, BS), 0)
    column = lax.broadcasted_iota(jnp.int32, (LOW, BS), 1)
    lower = pltpu.roll(gram[LOW:], LOW, 1)
    body = jnp.where((column >= LOW) | (row <= column), gram[:LOW], lower)
    diagonal = jnp.sum(jnp.where(row == column, lower, 0.0), axis=0, keepdims=True)
    return jnp.concatenate([body, jnp.broadcast_to(diagonal, (8, BS))], axis=0)


def unpacked(pack):
    row = lax.broadcasted_iota(jnp.int32, (LOW, BS), 0)
    column = lax.broadcasted_iota(jnp.int32, (LOW, BS), 1)
    body = pack[:LOW]
    turned = jnp.concatenate([body, jnp.zeros((LOW, BS), F32)], axis=0).T
    upper = jnp.where((column >= LOW) | (row <= column), body, turned[:LOW])
    lower = jnp.where(row > column, body, jnp.where(row == column, pack[LOW : LOW + 1], turned[:LOW]))
    lower = jnp.where(column < LOW, turned[LOW:], pltpu.roll(lower, LOW, 1))
    return jnp.concatenate([upper, lower], axis=0)


def three_parts(x):
    high = x.astype(BF16)
    rest = x - high.astype(F32)
    middle = rest.astype(BF16)
    low = (rest - middle.astype(F32)).astype(BF16)
    return high, middle, low


def inverse_factor(gram, work):
    n = BS
    rows = lax.broadcasted_iota(jnp.int32, (n, n), 0)
    columns = lax.broadcasted_iota(jnp.int32, (n, n), 1)
    work[:, :n] = gram
    work[:, n:] = jnp.where(rows == columns, 1.0, 0.0).astype(F32)
    place = lax.broadcasted_iota(jnp.int32, (PANEL, n), 0)
    for base in range(0, n, PANEL):
        panel = work[base : base + PANEL, :]
        left, right = panel[:, :n], panel[:, n:]
        spread = [
            jnp.broadcast_to(left[:, base + k : base + k + 1], (PANEL, n)) for k in range(PANEL)
        ]
        scale = jnp.zeros((PANEL, n), F32)
        for j in range(PANEL):
            inverse = 1.0 / spread[j][j : j + 1, :]
            scale = jnp.where(place == j, inverse, scale)
            if j + 1 < PANEL:
                factor = jnp.where(place > j, spread[j] * inverse, 0.0)
                for k in range(j + 1, PANEL):
                    spread[k] = spread[k] - factor * spread[k][j : j + 1, :]
                left = left - factor * left[j : j + 1, :]
                right = right - factor * right[j : j + 1, :]
        if base + PANEL < n:
            ah, am, al = three_parts(left * scale)
            both = jnp.concatenate([left, right], axis=1)
            bh, bm, bl = three_parts(both)
            update = lax.dot_general(
                jnp.concatenate([ah, ah, am, am, ah, al], axis=0),
                jnp.concatenate([bh, bm, bh, bm, bl, bh], axis=0),
                (((0,), (0,)), ((), ())),
                preferred_element_type=F32,
            )
            work[base + PANEL :, :] -= update[base + PANEL :, :]
        work[base : base + PANEL, n:] = right * jnp.sqrt(scale)


def solve_kernel(total_rows, meta, gram, split, out, work, result, sem):
    flip = meta[0, 0]
    inverse_factor(unpacked(gram[...]), work)
    spread = (work[:, BS:] * jnp.sqrt(F32(total_rows))).T
    high = spread.astype(BF16)
    low = (spread - high.astype(F32)).astype(BF16)
    half = jnp.concatenate([high, low], axis=1)
    factor = jnp.concatenate([half, half], axis=0)
    steps = 8
    size = OWN // steps
    copies = []
    for step in range(steps):
        rows = split[step * size : (step + 1) * size].reshape(size * BS, 2 * BS)
        product = jnp.dot(rows, factor, preferred_element_type=F32)
        result[step * size : (step + 1) * size] = (product[:, :BS] + product[:, BS:]).reshape(size, BS, BS)
        copies.append(
            pltpu.make_async_copy(
                result.at[pl.ds(step * size, size)], out.at[pl.ds(step * size ^ flip, size)], sem.at[step]
            )
        )
        copies[-1].start()
    for copy in copies:
        copy.wait()


def swap(pairs, x):
    return lax.ppermute(x, "node", pairs)


def sum_over_node(x, size):
    for masks in ((1,), (2, 6, 4), (8, 24, 16), (32, 64, 96), (224,)):
        x = x + sum(swap([(i, i ^ mask) for i in range(size)], x) for mask in masks)
    return x


def local(embed, tiles, tile_rows, tile_cols, tile_count):
    size = lax.axis_size("node")
    device = lax.axis_index("node")
    flip = (device % 2) * HALF
    to_chip = [(i, (i + 1) % size if i % 2 else (i - 1) % size) for i in range(size)]
    to_core = [(i, i ^ 1) for i in range(size)]
    blocks = embed.reshape(OWN, BS, BS)

    cross = lax.dynamic_slice_in_dim(blocks, flip, HALF, 0).astype(BF16)
    cross_in = swap(to_chip, cross)
    where = device.astype(jnp.int32).reshape(1)

    def load(*refs):
        load_kernel(size, *refs)

    blocks_f32 = vmem(OWN, BS, BS, dtype=F32)
    source = vmem(OWN, BS, BS, dtype=BF16)
    half = vmem(HALF, BS, BS, dtype=BF16)
    work = cost(2 * 96 * BS**3, 8 * MIB)
    brief = cost(2 * BS**3, BS * BS)
    total, kept, inner, order, meta = pl.pallas_call(
        load,
        out_shape=(
            blocks_f32,
            vmem(SLOTS + 1, BS, BS, dtype=BF16),
            half,
            vmem(1, 3 * LISTLEN, dtype=jnp.int32),
            vmem(1, LISTLEN, dtype=jnp.int32),
        ),
        in_specs=[S, S, M, M, M, M],
        out_specs=(V, V, V, V, V),
        scratch_shapes=[
            vmem(8, LISTLEN, dtype=jnp.int32),
            vmem(1, SLOTS, dtype=jnp.int32),
            vmem(1, SLOTS, dtype=jnp.int32),
            pltpu.SemaphoreType.DMA((4 + TILE_COPIES,)),
        ],
        compiler_params=params(24),
        cost_estimate=work,
        name="load",
    )(where, tile_count, *map(in_hbm, (tile_rows.reshape(1, SLOTS), tile_cols.reshape(1, SLOTS), blocks, tiles)))
    inner_in = swap(to_core, inner)

    total = pl.pallas_call(
        own_first_kernel,
        out_shape=blocks_f32,
        in_specs=[S, S, V, V, V, V],
        out_specs=V,
        input_output_aliases={5: 0},
        scratch_shapes=[source],
        compiler_params=params(24),
        cost_estimate=work,
        name="own_first",
    )(order, meta, in_vmem(cross), in_vmem(inner), in_vmem(kept), in_vmem(total))

    total, halo, cross = pl.pallas_call(
        halo_first_cross_kernel,
        out_shape=(blocks_f32, source, half),
        in_specs=[S, S, V, V, V, V],
        out_specs=(V, V, V),
        input_output_aliases={5: 0},
        compiler_params=params(24),
        cost_estimate=work,
        name="halo_first_cross",
    )(order, meta, in_vmem(cross_in), in_vmem(inner_in), in_vmem(kept), in_vmem(total))
    cross_in = swap(to_chip, cross)

    quarter = vmem(HALF // 2, BS, BS, dtype=BF16)
    total, lower, upper = pl.pallas_call(
        own_second_kernel,
        out_shape=(blocks_f32, quarter, quarter),
        in_specs=[S, S, V, V, V, V],
        out_specs=(V, V, V),
        input_output_aliases={5: 0},
        scratch_shapes=[source],
        compiler_params=params(24),
        cost_estimate=brief,
        name="own_second",
    )(order, meta, in_vmem(halo), in_vmem(cross), in_vmem(kept), in_vmem(total))
    lower_in, upper_in = swap(to_core, lower), swap(to_core, upper)

    split, gram = pl.pallas_call(
        halo_second_kernel,
        out_shape=(vmem(OWN, BS, 2 * BS, dtype=BF16), vmem(LOW + 8, BS, dtype=F32)),
        in_specs=[S, S, V, V, V, V, V, H],
        out_specs=(V, V),
        scratch_shapes=[source, blocks_f32, blocks_f32, pltpu.SemaphoreType.DMA((2,))],
        compiler_params=params(24),
        cost_estimate=work,
        name="halo_second",
    )(order, meta, *map(in_vmem, (cross_in, lower_in, upper_in, kept, total)), blocks)

    gram = sum_over_node(gram, size)

    def solve(*refs):
        solve_kernel(embed.shape[0] * size, *refs)

    out = pl.pallas_call(
        solve,
        out_shape=jax.ShapeDtypeStruct((OWN, BS, BS), F32),
        in_specs=[S, V, V],
        out_specs=H,
        scratch_shapes=[vmem(BS, 2 * BS, dtype=F32), blocks_f32, pltpu.SemaphoreType.DMA((8,))],
        compiler_params=params(24),
        name="solve",
    )(meta, in_vmem(gram), in_vmem(split))
    return out.reshape(embed.shape)


def solution(mesh):
    return jax.shard_map(
        local,
        mesh=mesh,
        in_specs=(P("node", None), P("node", None, None), P("node"), P("node"), P("node")),
        out_specs=P("node", None),
        check_vma=False,
    )
```

```python
import jax
import jax.numpy as jnp
from jax import lax
from jax.experimental import pallas as pl
from jax.experimental.pallas import tpu as pltpu
from jax.sharding import PartitionSpec as P

BS = 128
OWN = 32
HALF = 16
SLOTS = 192
LISTLEN = 256
GROUP = 8
PANEL = 16
TILE_COPIES = 8
CHUNK = 4
LOW = BS // 2
MIB = 1024 * 1024

F32 = jnp.float32
BF16 = jnp.bfloat16

spectral_shift = 0.5
weight_zero = 0.6
weight_one = -0.9
weight_two = 0.45
c_embed = weight_zero - weight_two
c_sum = 2.0 * weight_two
c_first = weight_one - c_sum * spectral_shift


def vmem(*shape, dtype):
    return pltpu.VMEM(shape, dtype)


def in_vmem(array):
    return pltpu.with_memory_space_constraint(array, pltpu.VMEM)


def in_hbm(array):
    return pltpu.with_memory_space_constraint(array, pltpu.HBM)


V = pl.BlockSpec(memory_space=pltpu.VMEM)
S = pl.BlockSpec(memory_space=pltpu.SMEM)
H = pl.BlockSpec(memory_space=pl.ANY)
M = pl.BlockSpec(memory_space=pltpu.HBM)


def params(mib):
    return pltpu.CompilerParams(vmem_limit_bytes=mib * MIB)


def cost(flops, moved):
    return pl.CostEstimate(flops=flops, bytes_accessed=moved, transcendentals=0)


def which_list(bucket):
    return (bucket >= OWN).astype(jnp.int32) + (bucket >= OWN + HALF).astype(jnp.int32)


def columns_of(row):
    return jnp.broadcast_to(row, (row.shape[1], row.shape[1])).T


def slot_lists(tile_rows, tile_cols, device, count, flip, size):
    i32 = jnp.int32
    shape = (1, LISTLEN)
    core = device % 2
    local = tile_cols - device * OWN + HALF
    local = jnp.where(local < 0, local + OWN * size, local)
    local = jnp.where(local >= OWN * size, local - OWN * size, local)
    own = (local >= HALF) & (local < HALF + OWN)
    after = (local >= HALF + OWN).astype(i32)
    source = jnp.where(own, (local - HALF) ^ flip, local - 48 * after + HALF * (after ^ core))
    row = tile_rows ^ flip
    slots = lax.broadcasted_iota(i32, shape, 1)
    alive = slots < count
    bucket = jnp.where(alive, jnp.where(own, row, row + OWN), 2 * OWN)
    kind = which_list(bucket)
    code = (slots | (source << 8) | (row << 16)).astype(F32)

    square = (LISTLEN, LISTLEN)
    before = lax.broadcasted_iota(i32, square, 0) < lax.broadcasted_iota(i32, square, 1)
    bucket_f32 = bucket.astype(F32)
    same = columns_of(bucket_f32) == jnp.broadcast_to(bucket_f32, square)
    rank = jnp.sum(jnp.where(same & before, 1.0, 0.0), axis=0, keepdims=True)
    wide = (2 * OWN, LISTLEN)
    buckets = lax.broadcasted_iota(i32, wide, 0)
    here = jnp.broadcast_to(bucket, wide)
    pairs = jnp.sum(jnp.where(buckets == here, 1.0, 0.0), axis=1, keepdims=True)
    pairs = jnp.floor((pairs + 1.0) * 0.5)
    kinds = which_list(buckets)
    earlier = (buckets < here) & (kinds == jnp.broadcast_to(kind, wide))
    start = jnp.sum(jnp.where(earlier, 2.0 * pairs, 0.0), axis=0, keepdims=True)
    place = jnp.where(alive, start + rank + (kind * LISTLEN).astype(F32), -1.0)
    place, code = columns_of(place), columns_of(code)
    lanes = lax.broadcasted_iota(i32, square, 1).astype(F32)
    order = [
        SLOTS + jnp.sum(jnp.where(place == lanes + k * LISTLEN, code - SLOTS, 0.0), axis=0, keepdims=True)
        for k in range(3)
    ]
    field = lax.broadcasted_iota(i32, wide, 1)
    meta = jnp.sum(jnp.where(kinds == field - 1, pairs, 0.0), axis=0, keepdims=True)
    meta = jnp.where(slots == 0, flip, meta.astype(i32))
    return jnp.concatenate(order, axis=1).astype(i32), meta


def tile_sums(order, start, stop, source, tiles, total):
    def group(g, carry):
        products = []
        for u in range(GROUP):
            at = start + 2 * (g * GROUP + u)
            first, second = order[0, at], order[0, at + 1]
            wide = jnp.concatenate([tiles[first & 255], tiles[second & 255]], axis=1)
            tall = jnp.concatenate([source[(first >> 8) & 255], source[(second >> 8) & 255]], axis=0)
            products.append((first >> 16, jnp.dot(wide, tall, preferred_element_type=F32)))
        for row, product in products:
            total[row] += product
        return carry

    lax.fori_loop(0, (stop + GROUP - 1) // GROUP, group, 0)


def load_kernel(size, where, counts, rows, columns, embed, tiles, total, kept, inner, order, meta, slots, near_rows, near_columns, sem):
    device, count = where[0], counts[0]
    flip = (device % 2) * HALF
    part = SLOTS // TILE_COPIES
    tile_copies = [
        pltpu.make_async_copy(
            tiles.at[pl.ds(c * part, part)], kept.at[pl.ds(c * part, part)], sem.at[2 + c]
        )
        for c in range(TILE_COPIES)
    ]
    halves = [
        pltpu.make_async_copy(
            embed.at[pl.ds(h * HALF ^ flip, HALF)], total.at[pl.ds(h * HALF, HALF)], sem.at[h]
        )
        for h in range(2)
    ]
    slot_copies = [
        pltpu.make_async_copy(rows, near_rows, sem.at[2 + TILE_COPIES]),
        pltpu.make_async_copy(columns, near_columns, sem.at[3 + TILE_COPIES]),
    ]
    for copy in slot_copies + halves + tile_copies:
        copy.start()
    kept[SLOTS] = jnp.zeros((BS, BS), BF16)
    slots[...] = jnp.zeros_like(slots)
    for copy in slot_copies:
        copy.wait()
    slots[0:1, :SLOTS] = near_rows[...]
    slots[1:2, :SLOTS] = near_columns[...]
    order[...], meta[...] = slot_lists(slots[0:1, :], slots[1:2, :], device, count, flip, size)
    for copy in halves:
        copy.wait()
    inner[...] = total[HALF:].astype(BF16)
    total[...] = total[...] * (-spectral_shift)
    for copy in tile_copies:
        copy.wait()


def own_first_kernel(order, meta, cross, inner, tiles, before, total, source):
    source[:HALF] = cross[...]
    source[HALF:] = inner[...]
    tile_sums(order, 0, meta[0, 1], source, tiles, total)


def halo_first_cross_kernel(order, meta, cross, inner, tiles, before, total, source, out_cross):
    source[:HALF] = cross[...]
    source[HALF:] = inner[...]
    tile_sums(order, LISTLEN, meta[0, 2], source, tiles, total)
    out_cross[...] = total[:HALF].astype(BF16)


def own_second_kernel(order, meta, halo, cross, tiles, before, total, out_lower, out_upper, source):
    tile_sums(order, 2 * LISTLEN, meta[0, 3], halo, tiles, total)
    inner = total[HALF:].astype(BF16)
    out_lower[...] = inner[: HALF // 2]
    out_upper[...] = inner[HALF // 2 :]
    source[:HALF] = cross[...]
    source[HALF:] = inner
    total[...] = total[...] * (c_first / c_sum)
    tile_sums(order, 0, meta[0, 1], source, tiles, total)


def halo_second_kernel(order, meta, cross, lower, upper, tiles, before, embed, split, gram, total, source, field, sem):
    flip = meta[0, 0]
    halves = [
        pltpu.make_async_copy(
            embed.at[pl.ds(h * HALF ^ flip, HALF)], field.at[pl.ds(h * HALF, HALF)], sem.at[h]
        )
        for h in range(2)
    ]
    for copy in halves:
        copy.start()
    source[:HALF] = cross[...]
    source[HALF : HALF + HALF // 2] = lower[...]
    source[HALF + HALF // 2 :] = upper[...]
    tile_sums(order, LISTLEN, meta[0, 2], source, tiles, total)
    tile_sums(order, 2 * LISTLEN, meta[0, 3], source, tiles, total)
    for copy in halves:
        copy.wait()

    sums = jnp.zeros((BS, 2 * BS), F32)
    for g in range(OWN // CHUNK):
        rows = pl.ds(g * CHUNK, CHUNK)
        mixed = (c_sum * total[rows] + c_embed * field[rows]).reshape(CHUNK * BS, BS)
        high = mixed.astype(BF16)
        low = (mixed - high.astype(F32)).astype(BF16)
        both = jnp.concatenate([high, low], axis=1)
        split[rows] = both.reshape(CHUNK, BS, 2 * BS)
        sums += lax.dot_general(high, both, (((0,), (0,)), ((), ())), preferred_element_type=F32)
    gram[...] = packed(sums[:, :BS] + (sums[:, BS:] + sums[:, BS:].T))


def packed(gram):
    row = lax.broadcasted_iota(jnp.int32, (LOW, BS), 0)
    column = lax.broadcasted_iota(jnp.int32, (LOW, BS), 1)
    lower = pltpu.roll(gram[LOW:], LOW, 1)
    body = jnp.where((column >= LOW) | (row <= column), gram[:LOW], lower)
    diagonal = jnp.sum(jnp.where(row == column, lower, 0.0), axis=0, keepdims=True)
    return jnp.concatenate([body, jnp.broadcast_to(diagonal, (8, BS))], axis=0)


def unpacked(pack):
    row = lax.broadcasted_iota(jnp.int32, (LOW, BS), 0)
    column = lax.broadcasted_iota(jnp.int32, (LOW, BS), 1)
    body = pack[:LOW]
    turned = jnp.concatenate([body, jnp.zeros((LOW, BS), F32)], axis=0).T
    upper = jnp.where((column >= LOW) | (row <= column), body, turned[:LOW])
    lower = jnp.where(row > column, body, jnp.where(row == column, pack[LOW : LOW + 1], turned[:LOW]))
    lower = jnp.where(column < LOW, turned[LOW:], pltpu.roll(lower, LOW, 1))
    return jnp.concatenate([upper, lower], axis=0)


def three_parts(x):
    high = x.astype(BF16)
    rest = x - high.astype(F32)
    middle = rest.astype(BF16)
    low = (rest - middle.astype(F32)).astype(BF16)
    return high, middle, low


def inverse_factor(gram, work):
    n = BS
    rows = lax.broadcasted_iota(jnp.int32, (n, n), 0)
    columns = lax.broadcasted_iota(jnp.int32, (n, n), 1)
    work[:, :n] = gram
    work[:, n:] = jnp.where(rows == columns, 1.0, 0.0).astype(F32)
    place = lax.broadcasted_iota(jnp.int32, (PANEL, n), 0)
    for base in range(0, n, PANEL):
        panel = work[base : base + PANEL, :]
        left, right = panel[:, :n], panel[:, n:]
        spread = [
            jnp.broadcast_to(left[:, base + k : base + k + 1], (PANEL, n)) for k in range(PANEL)
        ]
        scale = jnp.zeros((PANEL, n), F32)
        for j in range(PANEL):
            inverse = 1.0 / spread[j][j : j + 1, :]
            scale = jnp.where(place == j, inverse, scale)
            if j + 1 < PANEL:
                column = jnp.where(place > j, spread[j], 0.0)
                for k in range(j + 1, PANEL):
                    spread[k] = spread[k] - column * (spread[k][j : j + 1, :] * inverse)
                left = left - column * (left[j : j + 1, :] * inverse)
                right = right - column * (right[j : j + 1, :] * inverse)
        if base + PANEL < n:
            ah, am, al = three_parts(left * scale)
            both = jnp.concatenate([left, right], axis=1)
            bh, bm, bl = three_parts(both)
            update = lax.dot_general(
                jnp.concatenate([ah, ah, am, am, ah, al], axis=0),
                jnp.concatenate([bh, bm, bh, bm, bl, bh], axis=0),
                (((0,), (0,)), ((), ())),
                preferred_element_type=F32,
            )
            work[base + PANEL :, :] -= update[base + PANEL :, :]
        work[base : base + PANEL, n:] = right * jnp.sqrt(scale)


def solve_kernel(total_rows, meta, gram, split, out, work, result, sem):
    flip = meta[0, 0]
    inverse_factor(unpacked(gram[...]), work)
    spread = (work[:, BS:] * jnp.sqrt(F32(total_rows))).T
    high = spread.astype(BF16)
    low = (spread - high.astype(F32)).astype(BF16)
    half = jnp.concatenate([high, low], axis=1)
    factor = jnp.concatenate([half, half], axis=0)
    steps = 8
    size = OWN // steps
    copies = []
    for step in range(steps):
        rows = split[step * size : (step + 1) * size].reshape(size * BS, 2 * BS)
        product = jnp.dot(rows, factor, preferred_element_type=F32)
        result[step * size : (step + 1) * size] = (product[:, :BS] + product[:, BS:]).reshape(size, BS, BS)
        copies.append(
            pltpu.make_async_copy(
                result.at[pl.ds(step * size, size)], out.at[pl.ds(step * size ^ flip, size)], sem.at[step]
            )
        )
        copies[-1].start()
    for copy in copies:
        copy.wait()


def swap(pairs, x):
    return lax.ppermute(x, "node", pairs)


def sum_over_node(x, size):
    def masked(mask):
        return [(i, i ^ mask) for i in range(size)]

    def along_z(even, odd):
        plane = 32
        return [(i, (i + plane * (odd if i // plane % 2 else even)) % size) for i in range(size)]

    rounds = (
        (masked(1),),
        (masked(2), masked(6), masked(4)),
        (masked(8), masked(24), masked(16)),
        (along_z(1, -1), along_z(-1, 1), along_z(-2, 2)),
        (along_z(-3, 3),),
    )
    for pairs in rounds:
        x = x + sum(swap(pair, x) for pair in pairs)
    return x


def local(embed, tiles, tile_rows, tile_cols, tile_count):
    size = lax.axis_size("node")
    device = lax.axis_index("node")
    flip = (device % 2) * HALF
    to_chip = [(i, (i + 1) % size if i % 2 else (i - 1) % size) for i in range(size)]
    to_core = [(i, i ^ 1) for i in range(size)]
    blocks = embed.reshape(OWN, BS, BS)

    cross = lax.dynamic_slice_in_dim(blocks, flip, HALF, 0).astype(BF16)
    cross_in = swap(to_chip, cross)
    where = device.astype(jnp.int32).reshape(1)

    def load(*refs):
        load_kernel(size, *refs)

    blocks_f32 = vmem(OWN, BS, BS, dtype=F32)
    source = vmem(OWN, BS, BS, dtype=BF16)
    half = vmem(HALF, BS, BS, dtype=BF16)
    work = cost(2 * 96 * BS**3, 8 * MIB)
    brief = cost(2 * BS**3, BS * BS)
    total, kept, inner, order, meta = pl.pallas_call(
        load,
        out_shape=(
            blocks_f32,
            vmem(SLOTS + 1, BS, BS, dtype=BF16),
            half,
            vmem(1, 3 * LISTLEN, dtype=jnp.int32),
            vmem(1, LISTLEN, dtype=jnp.int32),
        ),
        in_specs=[S, S, M, M, M, M],
        out_specs=(V, V, V, V, V),
        scratch_shapes=[
            vmem(8, LISTLEN, dtype=jnp.int32),
            vmem(1, SLOTS, dtype=jnp.int32),
            vmem(1, SLOTS, dtype=jnp.int32),
            pltpu.SemaphoreType.DMA((4 + TILE_COPIES,)),
        ],
        compiler_params=params(24),
        cost_estimate=work,
        name="load",
    )(where, tile_count, *map(in_hbm, (tile_rows.reshape(1, SLOTS), tile_cols.reshape(1, SLOTS), blocks, tiles)))
    inner_in = swap(to_core, inner)

    total = pl.pallas_call(
        own_first_kernel,
        out_shape=blocks_f32,
        in_specs=[S, S, V, V, V, V],
        out_specs=V,
        input_output_aliases={5: 0},
        scratch_shapes=[source],
        compiler_params=params(24),
        cost_estimate=work,
        name="own_first",
    )(order, meta, in_vmem(cross), in_vmem(inner), in_vmem(kept), in_vmem(total))

    total, halo, cross = pl.pallas_call(
        halo_first_cross_kernel,
        out_shape=(blocks_f32, source, half),
        in_specs=[S, S, V, V, V, V],
        out_specs=(V, V, V),
        input_output_aliases={5: 0},
        compiler_params=params(24),
        cost_estimate=work,
        name="halo_first_cross",
    )(order, meta, in_vmem(cross_in), in_vmem(inner_in), in_vmem(kept), in_vmem(total))
    cross_in = swap(to_chip, cross)

    quarter = vmem(HALF // 2, BS, BS, dtype=BF16)
    total, lower, upper = pl.pallas_call(
        own_second_kernel,
        out_shape=(blocks_f32, quarter, quarter),
        in_specs=[S, S, V, V, V, V],
        out_specs=(V, V, V),
        input_output_aliases={5: 0},
        scratch_shapes=[source],
        compiler_params=params(24),
        cost_estimate=brief,
        name="own_second",
    )(order, meta, in_vmem(halo), in_vmem(cross), in_vmem(kept), in_vmem(total))
    lower_in, upper_in = swap(to_core, lower), swap(to_core, upper)

    split, gram, _ = pl.pallas_call(
        halo_second_kernel,
        out_shape=(vmem(OWN, BS, 2 * BS, dtype=BF16), vmem(LOW + 8, BS, dtype=F32), blocks_f32),
        in_specs=[S, S, V, V, V, V, V, H],
        out_specs=(V, V, V),
        input_output_aliases={6: 2},
        scratch_shapes=[source, blocks_f32, pltpu.SemaphoreType.DMA((2,))],
        compiler_params=params(24),
        cost_estimate=work,
        name="halo_second",
    )(order, meta, *map(in_vmem, (cross_in, lower_in, upper_in, kept, total)), blocks)

    gram = sum_over_node(gram, size)

    def solve(*refs):
        solve_kernel(embed.shape[0] * size, *refs)

    out = pl.pallas_call(
        solve,
        out_shape=jax.ShapeDtypeStruct((OWN, BS, BS), F32),
        in_specs=[S, V, V],
        out_specs=H,
        scratch_shapes=[vmem(BS, 2 * BS, dtype=F32), blocks_f32, pltpu.SemaphoreType.DMA((8,))],
        compiler_params=params(24),
        name="solve",
    )(meta, in_vmem(gram), in_vmem(split))
    return out.reshape(embed.shape)


def solution(mesh):
    return jax.shard_map(
        local,
        mesh=mesh,
        in_specs=(P("node", None), P("node", None, None), P("node"), P("node"), P("node")),
        out_specs=P("node", None),
        check_vma=False,
    )
```

```python
import jax
import jax.numpy as jnp
from jax import lax
from jax.experimental import pallas as pl
from jax.experimental.pallas import tpu as pltpu
from jax.sharding import PartitionSpec as P

BS = 128
OWN = 32
HALF = 16
SLOTS = 192
LISTLEN = 256
GROUP = 8
PANEL = 16
TILE_COPIES = 8
CHUNK = 8
LOW = BS // 2
MIB = 1024 * 1024

F32 = jnp.float32
BF16 = jnp.bfloat16

spectral_shift = 0.5
weight_zero = 0.6
weight_one = -0.9
weight_two = 0.45
c_embed = weight_zero - weight_two
c_sum = 2.0 * weight_two
c_first = weight_one - c_sum * spectral_shift


def vmem(*shape, dtype):
    return pltpu.VMEM(shape, dtype)


def in_vmem(array):
    return pltpu.with_memory_space_constraint(array, pltpu.VMEM)


def in_hbm(array):
    return pltpu.with_memory_space_constraint(array, pltpu.HBM)


V = pl.BlockSpec(memory_space=pltpu.VMEM)
S = pl.BlockSpec(memory_space=pltpu.SMEM)
H = pl.BlockSpec(memory_space=pl.ANY)
M = pl.BlockSpec(memory_space=pltpu.HBM)


def params(mib):
    return pltpu.CompilerParams(vmem_limit_bytes=mib * MIB)


def cost(flops, moved):
    return pl.CostEstimate(flops=flops, bytes_accessed=moved, transcendentals=0)


def which_list(bucket):
    return (bucket >= OWN).astype(jnp.int32) + (bucket >= OWN + HALF).astype(jnp.int32)


def columns_of(row):
    return jnp.broadcast_to(row, (row.shape[1], row.shape[1])).T


def slot_lists(tile_rows, tile_cols, device, count, flip, size):
    i32 = jnp.int32
    shape = (1, LISTLEN)
    core = device % 2
    local = tile_cols - device * OWN + HALF
    local = jnp.where(local < 0, local + OWN * size, local)
    local = jnp.where(local >= OWN * size, local - OWN * size, local)
    own = (local >= HALF) & (local < HALF + OWN)
    after = (local >= HALF + OWN).astype(i32)
    source = jnp.where(own, (local - HALF) ^ flip, local - 48 * after + HALF * (after ^ core))
    row = tile_rows ^ flip
    slots = lax.broadcasted_iota(i32, shape, 1)
    alive = slots < count
    bucket = jnp.where(alive, jnp.where(own, row, row + OWN), 2 * OWN)
    kind = which_list(bucket)
    code = (slots | (source << 8) | (row << 16)).astype(F32)

    square = (LISTLEN, LISTLEN)
    before = lax.broadcasted_iota(i32, square, 0) < lax.broadcasted_iota(i32, square, 1)
    bucket_f32 = bucket.astype(F32)
    same = columns_of(bucket_f32) == jnp.broadcast_to(bucket_f32, square)
    rank = jnp.sum(jnp.where(same & before, 1.0, 0.0), axis=0, keepdims=True)
    wide = (2 * OWN, LISTLEN)
    buckets = lax.broadcasted_iota(i32, wide, 0)
    here = jnp.broadcast_to(bucket, wide)
    pairs = jnp.sum(jnp.where(buckets == here, 1.0, 0.0), axis=1, keepdims=True)
    pairs = jnp.floor((pairs + 1.0) * 0.5)
    kinds = which_list(buckets)
    earlier = (buckets < here) & (kinds == jnp.broadcast_to(kind, wide))
    start = jnp.sum(jnp.where(earlier, 2.0 * pairs, 0.0), axis=0, keepdims=True)
    place = jnp.where(alive, start + rank + (kind * LISTLEN).astype(F32), -1.0)
    place, code = columns_of(place), columns_of(code)
    lanes = lax.broadcasted_iota(i32, square, 1).astype(F32)
    order = [
        SLOTS + jnp.sum(jnp.where(place == lanes + k * LISTLEN, code - SLOTS, 0.0), axis=0, keepdims=True)
        for k in range(3)
    ]
    field = lax.broadcasted_iota(i32, wide, 1)
    meta = jnp.sum(jnp.where(kinds == field - 1, pairs, 0.0), axis=0, keepdims=True)
    meta = jnp.where(slots == 0, flip, meta.astype(i32))
    return jnp.concatenate(order, axis=1).astype(i32), meta


def tile_sums(order, start, stop, source, tiles, total):
    def group(g, carry):
        products = []
        for u in range(GROUP):
            at = start + 2 * (g * GROUP + u)
            first, second = order[0, at], order[0, at + 1]
            wide = jnp.concatenate([tiles[first & 255], tiles[second & 255]], axis=1)
            tall = jnp.concatenate([source[(first >> 8) & 255], source[(second >> 8) & 255]], axis=0)
            products.append((first >> 16, jnp.dot(wide, tall, preferred_element_type=F32)))
        for row, product in products:
            total[row] += product
        return carry

    lax.fori_loop(0, (stop + GROUP - 1) // GROUP, group, 0)


def load_kernel(size, where, counts, rows, columns, embed, tiles, total, kept, inner, order, meta, slots, near_rows, near_columns, sem):
    device, count = where[0], counts[0]
    flip = (device % 2) * HALF
    part = SLOTS // TILE_COPIES
    tile_copies = [
        pltpu.make_async_copy(
            tiles.at[pl.ds(c * part, part)], kept.at[pl.ds(c * part, part)], sem.at[2 + c]
        )
        for c in range(TILE_COPIES)
    ]
    halves = [
        pltpu.make_async_copy(
            embed.at[pl.ds(h * HALF ^ flip, HALF)], total.at[pl.ds(h * HALF, HALF)], sem.at[h]
        )
        for h in range(2)
    ]
    slot_copies = [
        pltpu.make_async_copy(rows, near_rows, sem.at[2 + TILE_COPIES]),
        pltpu.make_async_copy(columns, near_columns, sem.at[3 + TILE_COPIES]),
    ]
    for copy in slot_copies + halves + tile_copies:
        copy.start()
    kept[SLOTS] = jnp.zeros((BS, BS), BF16)
    slots[...] = jnp.zeros_like(slots)
    for copy in slot_copies:
        copy.wait()
    slots[0:1, :SLOTS] = near_rows[...]
    slots[1:2, :SLOTS] = near_columns[...]
    order[...], meta[...] = slot_lists(slots[0:1, :], slots[1:2, :], device, count, flip, size)
    for copy in halves:
        copy.wait()
    inner[...] = total[HALF:].astype(BF16)
    total[...] = total[...] * (-spectral_shift)
    for copy in tile_copies:
        copy.wait()


def own_first_kernel(order, meta, cross, inner, tiles, before, total, source):
    source[:HALF] = cross[...]
    source[HALF:] = inner[...]
    tile_sums(order, 0, meta[0, 1], source, tiles, total)


def halo_first_cross_kernel(order, meta, cross, inner, tiles, before, total, source, out_cross):
    source[:HALF] = cross[...]
    source[HALF:] = inner[...]
    tile_sums(order, LISTLEN, meta[0, 2], source, tiles, total)
    out_cross[...] = total[:HALF].astype(BF16)


def own_second_kernel(order, meta, halo, cross, tiles, before, total, out_lower, out_upper, source):
    tile_sums(order, 2 * LISTLEN, meta[0, 3], halo, tiles, total)
    inner = total[HALF:].astype(BF16)
    out_lower[...] = inner[: HALF // 2]
    out_upper[...] = inner[HALF // 2 :]
    source[:HALF] = cross[...]
    source[HALF:] = inner
    total[...] = total[...] * (c_first / c_sum)
    tile_sums(order, 0, meta[0, 1], source, tiles, total)


def halo_second_kernel(order, meta, cross, lower, upper, tiles, before, embed, split, gram, total, source, field, sem):
    flip = meta[0, 0]
    halves = [
        pltpu.make_async_copy(
            embed.at[pl.ds(h * HALF ^ flip, HALF)], field.at[pl.ds(h * HALF, HALF)], sem.at[h]
        )
        for h in range(2)
    ]
    for copy in halves:
        copy.start()
    source[:HALF] = cross[...]
    source[HALF : HALF + HALF // 2] = lower[...]
    source[HALF + HALF // 2 :] = upper[...]
    tile_sums(order, LISTLEN, meta[0, 2], source, tiles, total)
    tile_sums(order, 2 * LISTLEN, meta[0, 3], source, tiles, total)
    for copy in halves:
        copy.wait()

    sums = jnp.zeros((BS, 2 * BS), F32)
    for g in range(OWN // CHUNK):
        rows = pl.ds(g * CHUNK, CHUNK)
        mixed = (c_sum * total[rows] + c_embed * field[rows]).reshape(CHUNK * BS, BS)
        high = mixed.astype(BF16)
        low = (mixed - high.astype(F32)).astype(BF16)
        both = jnp.concatenate([high, low], axis=1)
        split[rows] = both.reshape(CHUNK, BS, 2 * BS)
        sums += lax.dot_general(high, both, (((0,), (0,)), ((), ())), preferred_element_type=F32)
    gram[...] = packed(sums[:, :BS] + (sums[:, BS:] + sums[:, BS:].T))


def packed(gram):
    row = lax.broadcasted_iota(jnp.int32, (LOW, BS), 0)
    column = lax.broadcasted_iota(jnp.int32, (LOW, BS), 1)
    lower = pltpu.roll(gram[LOW:], LOW, 1)
    body = jnp.where((column >= LOW) | (row <= column), gram[:LOW], lower)
    diagonal = jnp.sum(jnp.where(row == column, lower, 0.0), axis=0, keepdims=True)
    return jnp.concatenate([body, jnp.broadcast_to(diagonal, (8, BS))], axis=0)


def unpacked(pack):
    row = lax.broadcasted_iota(jnp.int32, (LOW, BS), 0)
    column = lax.broadcasted_iota(jnp.int32, (LOW, BS), 1)
    body = pack[:LOW]
    turned = jnp.concatenate([body, jnp.zeros((LOW, BS), F32)], axis=0).T
    upper = jnp.where((column >= LOW) | (row <= column), body, turned[:LOW])
    lower = jnp.where(row > column, body, jnp.where(row == column, pack[LOW : LOW + 1], turned[:LOW]))
    lower = jnp.where(column < LOW, turned[LOW:], pltpu.roll(lower, LOW, 1))
    return jnp.concatenate([upper, lower], axis=0)


def three_parts(x):
    high = x.astype(BF16)
    rest = x - high.astype(F32)
    middle = rest.astype(BF16)
    low = (rest - middle.astype(F32)).astype(BF16)
    return high, middle, low


def inverse_factor(gram, work):
    n = BS
    rows = lax.broadcasted_iota(jnp.int32, (n, n), 0)
    columns = lax.broadcasted_iota(jnp.int32, (n, n), 1)
    work[:, :n] = gram
    work[:, n:] = jnp.where(rows == columns, 1.0, 0.0).astype(F32)
    place = lax.broadcasted_iota(jnp.int32, (PANEL, n), 0)
    for base in range(0, n, PANEL):
        panel = work[base : base + PANEL, :]
        left, right = panel[:, :n], panel[:, n:]
        spread = [
            jnp.broadcast_to(left[:, base + k : base + k + 1], (PANEL, n)) for k in range(PANEL)
        ]
        scale = jnp.zeros((PANEL, n), F32)
        for j in range(PANEL):
            inverse = 1.0 / spread[j][j : j + 1, :]
            scale = jnp.where(place == j, inverse, scale)
            if j + 1 < PANEL:
                column = jnp.where(place > j, spread[j], 0.0)
                for k in range(j + 1, PANEL):
                    spread[k] = spread[k] - column * (spread[k][j : j + 1, :] * inverse)
                left = left - column * (left[j : j + 1, :] * inverse)
                right = right - column * (right[j : j + 1, :] * inverse)
        if base + PANEL < n:
            ah, am, al = three_parts(left * scale)
            both = jnp.concatenate([left, right], axis=1)
            bh, bm, bl = three_parts(both)
            update = lax.dot_general(
                jnp.concatenate([ah, ah, am, am, ah, al], axis=0),
                jnp.concatenate([bh, bm, bh, bm, bl, bh], axis=0),
                (((0,), (0,)), ((), ())),
                preferred_element_type=F32,
            )
            work[base + PANEL :, :] -= update[base + PANEL :, :]
        work[base : base + PANEL, n:] = right * jnp.sqrt(scale)


def solve_kernel(total_rows, meta, gram, split, out, work, result, sem):
    flip = meta[0, 0]
    inverse_factor(unpacked(gram[...]), work)
    spread = (work[:, BS:] * jnp.sqrt(F32(total_rows))).T
    high = spread.astype(BF16)
    low = (spread - high.astype(F32)).astype(BF16)
    half = jnp.concatenate([high, low], axis=1)
    factor = jnp.concatenate([half, half], axis=0)
    steps = 8
    size = OWN // steps
    copies = []
    for step in range(steps):
        rows = split[step * size : (step + 1) * size].reshape(size * BS, 2 * BS)
        product = jnp.dot(rows, factor, preferred_element_type=F32)
        result[step * size : (step + 1) * size] = (product[:, :BS] + product[:, BS:]).reshape(size, BS, BS)
        copies.append(
            pltpu.make_async_copy(
                result.at[pl.ds(step * size, size)], out.at[pl.ds(step * size ^ flip, size)], sem.at[step]
            )
        )
        copies[-1].start()
    for copy in copies:
        copy.wait()


def swap(pairs, x):
    return lax.ppermute(x, "node", pairs)


def sum_over_node(x, size):
    def masked(mask):
        return [(i, i ^ mask) for i in range(size)]

    def along_z(even, odd):
        plane = 32
        return [(i, (i + plane * (odd if i // plane % 2 else even)) % size) for i in range(size)]

    rounds = (
        (masked(1),),
        (masked(2), masked(6), masked(4)),
        (masked(8), masked(24), masked(16)),
        (along_z(1, -1), along_z(-1, 1), along_z(-2, 2)),
        (along_z(-3, 3),),
    )
    for pairs in rounds:
        x = x + sum(swap(pair, x) for pair in pairs)
    return x


def local(embed, tiles, tile_rows, tile_cols, tile_count):
    size = lax.axis_size("node")
    device = lax.axis_index("node")
    flip = (device % 2) * HALF
    to_chip = [(i, (i + 1) % size if i % 2 else (i - 1) % size) for i in range(size)]
    to_core = [(i, i ^ 1) for i in range(size)]
    blocks = embed.reshape(OWN, BS, BS)

    cross = lax.dynamic_slice_in_dim(blocks, flip, HALF, 0).astype(BF16)
    cross_in = swap(to_chip, cross)
    where = device.astype(jnp.int32).reshape(1)

    def load(*refs):
        load_kernel(size, *refs)

    blocks_f32 = vmem(OWN, BS, BS, dtype=F32)
    source = vmem(OWN, BS, BS, dtype=BF16)
    half = vmem(HALF, BS, BS, dtype=BF16)
    work = cost(2 * 96 * BS**3, 8 * MIB)
    brief = cost(2 * BS**3, BS * BS)
    total, kept, inner, order, meta = pl.pallas_call(
        load,
        out_shape=(
            blocks_f32,
            vmem(SLOTS + 1, BS, BS, dtype=BF16),
            half,
            vmem(1, 3 * LISTLEN, dtype=jnp.int32),
            vmem(1, LISTLEN, dtype=jnp.int32),
        ),
        in_specs=[S, S, M, M, M, M],
        out_specs=(V, V, V, V, V),
        scratch_shapes=[
            vmem(8, LISTLEN, dtype=jnp.int32),
            vmem(1, SLOTS, dtype=jnp.int32),
            vmem(1, SLOTS, dtype=jnp.int32),
            pltpu.SemaphoreType.DMA((4 + TILE_COPIES,)),
        ],
        compiler_params=params(24),
        cost_estimate=work,
        name="load",
    )(where, tile_count, *map(in_hbm, (tile_rows.reshape(1, SLOTS), tile_cols.reshape(1, SLOTS), blocks, tiles)))
    inner_in = swap(to_core, inner)

    total = pl.pallas_call(
        own_first_kernel,
        out_shape=blocks_f32,
        in_specs=[S, S, V, V, V, V],
        out_specs=V,
        input_output_aliases={5: 0},
        scratch_shapes=[source],
        compiler_params=params(24),
        cost_estimate=work,
        name="own_first",
    )(order, meta, in_vmem(cross), in_vmem(inner), in_vmem(kept), in_vmem(total))

    total, halo, cross = pl.pallas_call(
        halo_first_cross_kernel,
        out_shape=(blocks_f32, source, half),
        in_specs=[S, S, V, V, V, V],
        out_specs=(V, V, V),
        input_output_aliases={5: 0},
        compiler_params=params(24),
        cost_estimate=work,
        name="halo_first_cross",
    )(order, meta, in_vmem(cross_in), in_vmem(inner_in), in_vmem(kept), in_vmem(total))
    cross_in = swap(to_chip, cross)

    quarter = vmem(HALF // 2, BS, BS, dtype=BF16)
    total, lower, upper = pl.pallas_call(
        own_second_kernel,
        out_shape=(blocks_f32, quarter, quarter),
        in_specs=[S, S, V, V, V, V],
        out_specs=(V, V, V),
        input_output_aliases={5: 0},
        scratch_shapes=[source],
        compiler_params=params(24),
        cost_estimate=brief,
        name="own_second",
    )(order, meta, in_vmem(halo), in_vmem(cross), in_vmem(kept), in_vmem(total))
    lower_in, upper_in = swap(to_core, lower), swap(to_core, upper)

    split, gram, _ = pl.pallas_call(
        halo_second_kernel,
        out_shape=(vmem(OWN, BS, 2 * BS, dtype=BF16), vmem(LOW + 8, BS, dtype=F32), blocks_f32),
        in_specs=[S, S, V, V, V, V, V, H],
        out_specs=(V, V, V),
        input_output_aliases={6: 2},
        scratch_shapes=[source, blocks_f32, pltpu.SemaphoreType.DMA((2,))],
        compiler_params=params(24),
        cost_estimate=work,
        name="halo_second",
    )(order, meta, *map(in_vmem, (cross_in, lower_in, upper_in, kept, total)), blocks)

    gram = sum_over_node(gram, size)

    def solve(*refs):
        solve_kernel(embed.shape[0] * size, *refs)

    out = pl.pallas_call(
        solve,
        out_shape=jax.ShapeDtypeStruct((OWN, BS, BS), F32),
        in_specs=[S, V, V],
        out_specs=H,
        scratch_shapes=[vmem(BS, 2 * BS, dtype=F32), blocks_f32, pltpu.SemaphoreType.DMA((8,))],
        compiler_params=params(24),
        name="solve",
    )(meta, in_vmem(gram), in_vmem(split))
    return out.reshape(embed.shape)


def solution(mesh):
    return jax.shard_map(
        local,
        mesh=mesh,
        in_specs=(P("node", None), P("node", None, None), P("node"), P("node"), P("node")),
        out_specs=P("node", None),
        check_vma=False,
    )
```
